32 devices in a mesh: tile: 4 (over z), dir: 8 (over y, x, core).
Axes of the slice: x: 2, y: 2, z: 4, core: 2. Of those that a mesh axis runs over, the one named last changes fastest.
Arguments:
- spectrum: float32 [48, 36, 8192], P('dir', None, 'tile'), may hold values from 0.2 to 5
- active_points: int32 [4], P('tile'), may hold values from 1024 to 2048, as said below
- send_list: int32 [4, 4, 128], P('tile'), may hold values from 0 to 2047, as said below
- neighbor: int32 [4, 8192], P(None, 'tile'), may hold values from 0 to 2559, as said below
- depth_class: int32 [8192], P('tile'), may hold values from 0 to 3
- group_speed: float32 [4, 36], replicated, may hold values from 0.05 to 0.35
- refraction: float32 [8192], P('tile'), may hold values from -0.45 to 0.45
- kernel: float32 [1728, 1728], P('dir'), may hold values from -0.078125 to 0.078125
- wave_weight: float32 [36], replicated, may hold values from 5e-05 to 0.0005
Outputs:
- new_spectrum: float32 [48, 36, 8192], P('dir', None, 'tile')
The draws below stay inside these ranges and needn't reach their ends.
Inputs may be any that keep to these rules, and one draw needn't show every extreme that they name: `active_points`: at least one tile has all 2048 points in use. send_list[s, t, j] is a point number within tile s. `neighbor`: a value v below 2048 names point v of the same tile; v = 2048 + s * 128 + j names the point send_list[s, t, j] of tile s.
All inputs are finite; a program needn't handle non-finite values.
Results may differ from the reference program's by a relative error of at most 0.0001.
Values sent between devices are 32-bit elements; how exact they have to be, the bound alone decides.
A program may use at most 128 MiB of HBM per device.

```python
import math
import jax
import jax.numpy as jnp
from jax import lax

DIRS = 48
FREQS = 36
CLASSES = 4
P_DEV = 2048
FACE = 128
SUB = 5
TILES = 4
POINTS = 8192
SPEC = 1728


def draw_active_points(key, part):
    counts = jax.random.randint(key, (TILES,), P_DEV // 2, P_DEV + 1)
    chosen = jax.random.randint(jax.random.fold_in(key, 11), (), 0, TILES)
    return jnp.where(jnp.arange(TILES) == chosen, P_DEV, counts).astype(jnp.int32)


def draw_send_list(key, part):
    return jax.random.randint(key, (TILES, TILES, FACE), 0, P_DEV).astype(jnp.int32)


def draw_neighbor(key, part):
    local_links = jax.random.randint(jax.random.fold_in(key, 21), (4, POINTS), 0, P_DEV)
    remote_links = P_DEV + jax.random.randint(jax.random.fold_in(key, 22), (4, POINTS), 0, TILES * FACE)
    picker = jax.random.randint(jax.random.fold_in(key, 23), (4, POINTS), 0, 4)
    return jnp.where(picker == 0, remote_links, local_links).astype(jnp.int32)


def place_ends(drawn, own_key, low, high):
    spot = [jax.random.randint(jax.random.fold_in(own_key, axis), (), 0, length) for axis, length in enumerate(drawn.shape)]
    main_axis = drawn.shape.index(max(drawn.shape))
    next_to = spot[:main_axis] + [(spot[main_axis] + 1) % drawn.shape[main_axis]] + spot[main_axis + 1:]
    return drawn.at[tuple(spot)].set(low).at[tuple(next_to)].set(high)


def block_scale(stream_key, extent, cuts, smallest, top_value):
    factor_of = 1.0
    for dim, parts in cuts:
        draws = jax.random.uniform(jax.random.fold_in(jax.random.fold_in(stream_key, 6), dim), (parts,), jnp.float32, smallest / len(cuts), top_value / len(cuts))
        factor_of = factor_of * jnp.repeat(jnp.exp(draws), extent[dim] // parts).reshape((-1,) + (1,) * (len(extent) - 1 - dim))
    return factor_of


def normal_values(own_key, dims, deviation, bound, shards=(), held_as=jnp.bfloat16):
    entries = jax.random.normal(own_key, dims, jnp.float32) * deviation
    if len(shards) > 0:
        entries = block_scale(own_key, dims, shards, -0.22, 0.18) * entries
    return jnp.clip(entries, min=-bound, max=bound).astype(held_as)


def setup_inputs(seed: int = 0) -> dict:
    seeds = jax.random.split(jax.random.key(seed), 10)
    return {
        "spectrum": jnp.clip(jnp.exp(math.log(5.0) - 3.218876 * jax.random.uniform(seeds[0], (DIRS, FREQS, POINTS), jnp.float32) ** block_scale(seeds[0], (DIRS, FREQS, POINTS), ((0, 8), (2, 4)), -0.2, 0.2)), 0.2, 5.0),
        "active_points": draw_active_points(jax.random.fold_in(seeds[9], 71), 0),
        "send_list": draw_send_list(jax.random.fold_in(seeds[9], 71), 0),
        "neighbor": draw_neighbor(jax.random.fold_in(seeds[9], 71), 0),
        "depth_class": place_ends(jax.random.randint(seeds[4], (POINTS,), 0, CLASSES), jax.random.fold_in(seeds[4], 1), 0, CLASSES - 1).astype(jnp.int32),
        "group_speed": jnp.clip(jax.random.uniform(seeds[5], (CLASSES, FREQS), jnp.float32, 0.05, 0.35), 0.05, 0.35),
        "refraction": jnp.clip(jax.random.uniform(seeds[6], (POINTS,), jnp.float32, -0.45, 0.45) * block_scale(seeds[6], (POINTS,), ((0, 4),), -0.4, 0.0), -0.45, 0.45),
        "kernel": normal_values(seeds[7], (SPEC, SPEC), (4 * DIRS * FREQS) ** -0.5, 0.078125, ((0, 8),), jnp.float32),
        "wave_weight": jnp.clip(jnp.exp(jax.random.uniform(seeds[8], (FREQS,), jnp.float32, math.log(4.999999873689376e-05), math.log(0.0005))), 4.999999873689376e-05, 0.0005),
    }


def reference(spectrum, active_points, send_list, neighbor, depth_class, group_speed, refraction, kernel, wave_weight):
    positions = jnp.arange(POINTS, dtype=jnp.int32)
    mask = (positions % P_DEV < active_points[positions // P_DEV]).astype(jnp.float32)
    field = spectrum * mask[None, None, :]
    theta = jnp.arange(DIRS).astype(jnp.float32) * (2.0 * math.pi / DIRS)
    angles = jnp.arange(4).astype(jnp.float32) * (math.pi / 2.0)
    upwind = jnp.maximum(jnp.cos(theta[:, None] - angles[None, :]), 0.0)
    onehot = (depth_class[None, :] == jnp.arange(CLASSES, dtype=jnp.int32)[:, None]).astype(jnp.float32)
    courant = jnp.sum(group_speed[:, :, None] * onehot[:, None, :], axis=0)
    pieces = []
    for tile in range(TILES):
        own = field[:, :, tile * P_DEV:(tile + 1) * P_DEV]
        received = [jnp.take(field[:, :, source * P_DEV:(source + 1) * P_DEV], send_list[source, tile], axis=2) for source in range(TILES)]
        extended = jnp.concatenate([own] + received, axis=2)
        links = neighbor[:, tile * P_DEV:(tile + 1) * P_DEV]
        flow = jnp.zeros_like(own)
        for which in range(4):
            flow = flow + upwind[:, which][:, None, None] * (jnp.take(extended, links[which], axis=2) - own)
        pieces.append(own + courant[None, :, tile * P_DEV:(tile + 1) * P_DEV] * flow)
    moved = jnp.concatenate(pieces, axis=2)
    lower = jnp.roll(moved, 1, axis=0)
    upper = jnp.roll(moved, -1, axis=0)
    forward = jnp.maximum(refraction, 0.0)[None, None, :]
    backward = jnp.maximum(-refraction, 0.0)[None, None, :]
    turned = moved + forward * (lower - moved) + backward * (upper - moved)
    state = turned.reshape(DIRS * FREQS, POINTS)
    weights_rows = jnp.tile(wave_weight, DIRS)
    for step in range(SUB):
        steep = jnp.sum(weights_rows[:, None] * state * state, axis=0)
        state = (state + jnp.dot(kernel, state, precision=lax.Precision.HIGHEST, preferred_element_type=jnp.float32)) / (1.0 + steep)[None, :]
    return state.reshape(DIRS, FREQS, POINTS) * mask[None, None, :]
```

```python
import functools
import math

import jax
import jax.numpy as jnp
from jax import lax
from jax.experimental import pallas as pl
from jax.experimental.pallas import tpu as pltpu
from jax.sharding import PartitionSpec as P

SUB = 5
F32 = jnp.float32
BF16 = jnp.bfloat16


def split2(x):
    hi = x.astype(BF16)
    return hi, (x - hi.astype(F32)).astype(BF16)


def pick_kernel(ext_ref, send_ref, out_ref):
    points = ext_ref.shape[1]
    want = lax.broadcasted_iota(jnp.int32, (points, send_ref.shape[1]), 0)
    pick = jnp.where(want == send_ref[...], 1.0, 0.0).astype(BF16)
    total = None
    rest = ext_ref[...]
    for _ in range(3):
        part = rest.astype(BF16)
        rest = rest - part.astype(F32)
        got = jnp.dot(part, pick, preferred_element_type=F32)
        total = got if total is None else total + got
    out_ref[...] = total


def move_kernel(ways, field_ref, halo_ref, idx_ref, up_ref, depth_ref, speed_ref, block_ref, out_ref, parts_ref):
    rows, points = field_ref.shape
    width = points + halo_ref.shape[1]

    @pl.when(pl.program_id(0) == 0)
    def _():
        for ref, lo in ((field_ref, 0), (halo_ref, points)):
            hi_part, lo_part = split2(ref[...])
            parts_ref[0, :, lo:lo + ref.shape[1]] = hi_part
            parts_ref[1, :, lo:lo + ref.shape[1]] = lo_part

    own = block_ref[...]
    cols = own.shape[1]
    number = lax.broadcasted_iota(jnp.int32, (width, cols), 0)
    flow = None
    for k in range(ways):
        pick = jnp.where(number == idx_ref[k:k + 1, :], 1.0, 0.0).astype(BF16)
        got = jnp.dot(parts_ref[0], pick, preferred_element_type=F32)
        got = got + jnp.dot(parts_ref[1], pick, preferred_element_type=F32)
        term = up_ref[:, k:k + 1] * (got - own)
        flow = term if flow is None else flow + term
    courant = None
    for c in range(speed_ref.shape[1]):
        term = speed_ref[:, c:c + 1] * jnp.where(depth_ref[...] == c, 1.0, 0.0)
        courant = term if courant is None else courant + term
    out_ref[0] = own + courant * flow


def source_kernel(freqs, blocks, moved_ref, turn_ref, mask_ref, weight_ref, kernel_ref, out_ref, khi_ref, klo_ref, shi_ref, slo_ref):
    count, points = out_ref.shape
    size = count // blocks

    @pl.loop(0, blocks)
    def _(i):
        rows = pl.ds(pl.multiple_of(i * size, size), size)
        hi, lo = split2(kernel_ref[rows, :])
        khi_ref[rows, :] = hi
        klo_ref[rows, :] = lo

    moved = moved_ref[...]
    forward = jnp.maximum(turn_ref[...], 0.0)
    backward = jnp.maximum(-turn_ref[...], 0.0)
    lower = pltpu.roll(moved, freqs, 0)
    upper = pltpu.roll(moved, count - freqs, 0)
    out_ref[...] = moved + forward * (lower - moved) + backward * (upper - moved)
    for step in range(SUB):
        state = out_ref[...]
        steep = jnp.sum(weight_ref[...] * (state * state), axis=0, keepdims=True)
        scale = 1.0 / (1.0 + steep)
        if step == SUB - 1:
            scale = scale * mask_ref[...]
        hi, lo = split2(state)
        shi_ref[...] = hi
        slo_ref[...] = lo

        @pl.loop(0, blocks)
        def _(i):
            rows = pl.ds(pl.multiple_of(i * size, size), size)
            khi = khi_ref[rows, :]
            product = jnp.dot(khi, shi_ref[...], preferred_element_type=F32)
            product = product + jnp.dot(khi, slo_ref[...], preferred_element_type=F32)
            product = product + jnp.dot(klo_ref[rows, :], shi_ref[...], preferred_element_type=F32)
            out_ref[rows, :] = (out_ref[rows, :] + product) * scale


def per_device(
    spectrum,
    active_points,
    send_list,
    neighbor,
    depth_class,
    group_speed,
    refraction,
    kernel,
    wave_weight,
):
    dirs_local, freqs, points = spectrum.shape
    tiles = lax.axis_size("tile")
    groups = lax.axis_size("dir")
    faces = send_list.shape[2]
    classes = group_speed.shape[0]
    rows = dirs_local * freqs
    count = rows * groups
    cols = points // groups
    total_dirs = dirs_local * groups
    group = lax.axis_index("dir")
    vmem = pltpu.CompilerParams(vmem_limit_bytes=56 * 2**20)
    whole = functools.partial(pl.BlockSpec, memory_space=pltpu.VMEM)

    full = lax.all_gather(kernel, "dir", axis=0, tiled=True)

    mask = (jnp.arange(points, dtype=jnp.int32) < active_points[0]).astype(F32)
    field = spectrum.reshape(rows, points) * mask[None, :]
    send = send_list.reshape(1, tiles * faces)
    outgoing = pl.pallas_call(
        pick_kernel,
        out_shape=jax.ShapeDtypeStruct((rows, tiles * faces), F32),
        in_specs=[whole(), whole()],
        out_specs=whole(),
        compiler_params=vmem,
        name="pick",
    )(field, send)
    incoming = lax.all_to_all(outgoing, "tile", split_axis=1, concat_axis=1, tiled=True)

    first_dir = group * dirs_local
    theta = (first_dir + jnp.arange(dirs_local, dtype=jnp.int32)).astype(F32) * (2.0 * math.pi / total_dirs)
    angles = jnp.arange(4).astype(F32) * (math.pi / 2.0)
    upwind = jnp.maximum(jnp.cos(theta[:, None] - angles[None, :]), 0.0)
    links = neighbor
    ways = 4
    quarter = total_dirs // 4
    if total_dirs % 4 == 0 and quarter % dirs_local == 0:
        k0 = first_dir // quarter
        pair = jnp.stack([k0, (k0 + 1) % 4])
        upwind = jnp.take(upwind, pair, axis=1)
        links = jnp.take(neighbor, pair, axis=0)
        ways = 2
    up_rows = jnp.repeat(upwind, freqs, axis=0)
    speed_rows = jnp.tile(group_speed.T, (dirs_local, 1))

    moved = pl.pallas_call(
        functools.partial(move_kernel, ways),
        grid=(groups,),
        out_shape=jax.ShapeDtypeStruct((groups, rows, cols), F32),
        in_specs=[
            whole(),
            whole(),
            pl.BlockSpec((ways, cols), lambda i: (0, i)),
            whole(),
            pl.BlockSpec((1, cols), lambda i: (0, i)),
            whole(),
            pl.BlockSpec((rows, cols), lambda i: (0, i)),
        ],
        out_specs=pl.BlockSpec((1, rows, cols), lambda i: (i, 0, 0)),
        scratch_shapes=[pltpu.VMEM((2, rows, points + tiles * faces), BF16)],
        compiler_params=vmem,
        name="move",
    )(field, incoming, links, up_rows, depth_class[None, :], speed_rows, field)

    mine = lax.all_to_all(moved, "dir", split_axis=0, concat_axis=0, tiled=True)
    start = group * cols
    turn = lax.dynamic_slice_in_dim(refraction, start, cols)[None, :]
    my_mask = lax.dynamic_slice_in_dim(mask, start, cols)[None, :]
    weights = jnp.tile(wave_weight, total_dirs)[:, None]
    blocks = 2
    state = pl.pallas_call(
        functools.partial(source_kernel, freqs, blocks),
        out_shape=jax.ShapeDtypeStruct((count, cols), F32),
        in_specs=[whole()] * 5,
        out_specs=whole(),
        scratch_shapes=[
            pltpu.VMEM((count, count), BF16),
            pltpu.VMEM((count, count), BF16),
            pltpu.VMEM((count, cols), BF16),
            pltpu.VMEM((count, cols), BF16),
        ],
        compiler_params=vmem,
        name="source",
    )(mine.reshape(count, cols), turn, my_mask, weights, full)
    back = lax.all_to_all(state.reshape(groups, rows, cols), "dir", split_axis=0, concat_axis=0, tiled=True)
    return jnp.transpose(back, (1, 0, 2)).reshape(dirs_local, freqs, points)


def solution(mesh):
    return jax.shard_map(
        per_device,
        mesh=mesh,
        in_specs=(
            P("dir", None, "tile"),
            P("tile"),
            P("tile", None, None),
            P(None, "tile"),
            P("tile"),
            P(),
            P("tile"),
            P("dir", None),
            P(),
        ),
        out_specs=P("dir", None, "tile"),
        check_vma=False,
    )
```

```python
import functools
import math

import jax
import jax.numpy as jnp
from jax import lax
from jax.experimental import pallas as pl
from jax.experimental.pallas import tpu as pltpu
from jax.sharding import PartitionSpec as P

SUB = 5
F32 = jnp.float32
BF16 = jnp.bfloat16


def split2(x):
    hi = x.astype(BF16)
    return hi, (x - hi.astype(F32)).astype(BF16)


def pick_kernel(ext_ref, send_ref, out_ref):
    points = ext_ref.shape[1]
    want = lax.broadcasted_iota(jnp.int32, (points, send_ref.shape[1]), 0)
    pick = jnp.where(want == send_ref[...], 1.0, 0.0).astype(BF16)
    total = None
    rest = ext_ref[...]
    for _ in range(3):
        part = rest.astype(BF16)
        rest = rest - part.astype(F32)
        got = jnp.dot(part, pick, preferred_element_type=F32)
        total = got if total is None else total + got
    out_ref[...] = total


def move_kernel(ways, field_ref, halo_ref, idx_ref, up_ref, depth_ref, speed_ref, block_ref, out_ref, parts_ref):
    rows, points = field_ref.shape
    width = points + halo_ref.shape[1]

    @pl.when(pl.program_id(0) == 0)
    def _():
        for ref, lo in ((field_ref, 0), (halo_ref, points)):
            hi_part, lo_part = split2(ref[...])
            parts_ref[0, :, lo:lo + ref.shape[1]] = hi_part
            parts_ref[1, :, lo:lo + ref.shape[1]] = lo_part

    own = block_ref[...]
    cols = own.shape[1]
    number = lax.broadcasted_iota(jnp.int32, (width, cols), 0)
    flow = None
    for k in range(ways):
        pick = jnp.where(number == idx_ref[k:k + 1, :], 1.0, 0.0).astype(BF16)
        got = jnp.dot(parts_ref[0], pick, preferred_element_type=F32)
        got = got + jnp.dot(parts_ref[1], pick, preferred_element_type=F32)
        term = up_ref[:, k:k + 1] * (got - own)
        flow = term if flow is None else flow + term
    courant = None
    for c in range(speed_ref.shape[1]):
        term = speed_ref[:, c:c + 1] * jnp.where(depth_ref[...] == c, 1.0, 0.0)
        courant = term if courant is None else courant + term
    out_ref[0] = own + courant * flow


def source_kernel(
    freqs, groups, moved_ref, turn_ref, mask_ref, weight_ref, half_ref, out_ref,
    other_ref, khi_ref, klo_ref, state_ref, shi_ref, slo_ref, done_ref,
    half_send, half_recv, send_sem, recv_sem,
):
    count, points = state_ref.shape
    rows = count // groups
    half = count // 2
    size = half // 2
    me = lax.axis_index("dir")
    parity = lax.rem(me, 2)
    twin = me + 1 - 2 * parity

    barrier = pltpu.get_barrier_semaphore()
    for r in range(1, groups):
        pl.semaphore_signal(barrier, inc=1, device_id={"dir": lax.rem(me + r, groups)}, device_id_type=pl.DeviceIdType.MESH)
    pl.semaphore_wait(barrier, groups - 1)

    copies = []
    for i in range(2):
        copy = pltpu.make_async_remote_copy(
            src_ref=half_ref.at[pl.ds(i * size, size)],
            dst_ref=other_ref.at[pl.ds(i * size, size)],
            send_sem=half_send.at[i],
            recv_sem=half_recv.at[i],
            device_id={"dir": twin},
            device_id_type=pl.DeviceIdType.MESH,
        )
        copy.start()
        copies.append(copy)

    def split_rows(ref, i, base):
        hi, lo = split2(ref[i * size:(i + 1) * size, :])
        to = pl.ds(pl.multiple_of(base * half + i * size, 16), size)
        khi_ref[to, :] = hi
        klo_ref[to, :] = lo

    moved = moved_ref[...]
    forward = jnp.maximum(turn_ref[...], 0.0)
    backward = jnp.maximum(-turn_ref[...], 0.0)
    lower = pltpu.roll(moved, freqs, 0)
    upper = pltpu.roll(moved, count - freqs, 0)
    state_ref[...] = moved + forward * (lower - moved) + backward * (upper - moved)
    for i in range(2):
        split_rows(half_ref, i, parity)
    for i in range(2):
        copies[i].wait()
        split_rows(other_ref, i, 1 - parity)

    def send(target):
        return pltpu.make_async_remote_copy(
            src_ref=done_ref.at[target],
            dst_ref=out_ref.at[:, pl.ds(pl.multiple_of(me * points, points), points)],
            send_sem=send_sem.at[target],
            recv_sem=recv_sem.at[me],
            device_id={"dir": target},
            device_id_type=pl.DeviceIdType.MESH,
        )

    def substep(last):
        state = state_ref[...]
        steep = jnp.sum(weight_ref[...] * (state * state), axis=0, keepdims=True)
        scale = 1.0 / (1.0 + steep)
        if last:
            scale = scale * mask_ref[...]
        hi, lo = split2(state)
        shi_ref[...] = hi
        slo_ref[...] = lo
        for h in range(2):
            khi = khi_ref[h * half:(h + 1) * half, :]
            product = jnp.dot(khi, shi_ref[...], preferred_element_type=F32)
            product = product + jnp.dot(khi, slo_ref[...], preferred_element_type=F32)
            product = product + jnp.dot(klo_ref[h * half:(h + 1) * half, :], shi_ref[...], preferred_element_type=F32)
            for j in range(groups // 2):
                d = 2 * j + h
                value = (state_ref[d * rows:(d + 1) * rows, :] + product[j * rows:(j + 1) * rows]) * scale
                if last:
                    done_ref[d] = value
                else:
                    state_ref[d * rows:(d + 1) * rows, :] = value
            if last:
                for j in range(groups // 2):
                    target = 2 * lax.rem(me // 2 + 1 + j, groups // 2) + h

                    @pl.when(target != me)
                    def _():
                        send(target).start()

    @pl.loop(0, SUB - 1)
    def _(step):
        substep(False)

    substep(True)
    out_ref[:, pl.ds(pl.multiple_of(me * points, points), points)] = done_ref[me]
    for r in range(1, groups):
        other = lax.rem(me + r, groups)
        send(other).wait_send()
        pltpu.make_async_remote_copy(
            src_ref=done_ref.at[other],
            dst_ref=out_ref.at[:, pl.ds(pl.multiple_of(other * points, points), points)],
            send_sem=send_sem.at[other],
            recv_sem=recv_sem.at[other],
            device_id={"dir": other},
            device_id_type=pl.DeviceIdType.MESH,
        ).wait_recv()


def per_device(
    spectrum,
    active_points,
    send_list,
    neighbor,
    depth_class,
    group_speed,
    refraction,
    kernel,
    wave_weight,
):
    dirs_local, freqs, points = spectrum.shape
    tiles = lax.axis_size("tile")
    groups = lax.axis_size("dir")
    faces = send_list.shape[2]
    classes = group_speed.shape[0]
    rows = dirs_local * freqs
    count = rows * groups
    cols = points // groups
    total_dirs = dirs_local * groups
    group = lax.axis_index("dir")
    vmem = pltpu.CompilerParams(vmem_limit_bytes=56 * 2**20)
    whole = functools.partial(pl.BlockSpec, memory_space=pltpu.VMEM)

    pairing = [list(range(c, groups, 2)) for c in range(2)]
    half = lax.all_gather(kernel, "dir", axis=0, tiled=True, axis_index_groups=pairing)

    mask = (jnp.arange(points, dtype=jnp.int32) < active_points[0]).astype(F32)
    field = spectrum.reshape(rows, points) * mask[None, :]
    send = send_list.reshape(1, tiles * faces)
    outgoing = pl.pallas_call(
        pick_kernel,
        out_shape=jax.ShapeDtypeStruct((rows, tiles * faces), F32),
        in_specs=[whole(), whole()],
        out_specs=whole(),
        compiler_params=vmem,
        name="pick",
    )(field, send)
    incoming = lax.all_to_all(outgoing, "tile", split_axis=1, concat_axis=1, tiled=True)

    first_dir = group * dirs_local
    theta = (first_dir + jnp.arange(dirs_local, dtype=jnp.int32)).astype(F32) * (2.0 * math.pi / total_dirs)
    angles = jnp.arange(4).astype(F32) * (math.pi / 2.0)
    upwind = jnp.maximum(jnp.cos(theta[:, None] - angles[None, :]), 0.0)
    links = neighbor
    ways = 4
    quarter = total_dirs // 4
    if total_dirs % 4 == 0 and quarter % dirs_local == 0:
        k0 = first_dir // quarter
        pair = jnp.stack([k0, (k0 + 1) % 4])
        upwind = jnp.take(upwind, pair, axis=1)
        links = jnp.take(neighbor, pair, axis=0)
        ways = 2
    up_rows = jnp.repeat(upwind, freqs, axis=0)
    speed_rows = jnp.tile(group_speed.T, (dirs_local, 1))

    moved = pl.pallas_call(
        functools.partial(move_kernel, ways),
        grid=(groups,),
        out_shape=jax.ShapeDtypeStruct((groups, rows, cols), F32),
        in_specs=[
            whole(),
            whole(),
            pl.BlockSpec((ways, cols), lambda i: (0, i)),
            whole(),
            pl.BlockSpec((1, cols), lambda i: (0, i)),
            whole(),
            pl.BlockSpec((rows, cols), lambda i: (0, i)),
        ],
        out_specs=pl.BlockSpec((1, rows, cols), lambda i: (i, 0, 0)),
        scratch_shapes=[pltpu.VMEM((2, rows, points + tiles * faces), BF16)],
        compiler_params=vmem,
        name="move",
    )(field, incoming, links, up_rows, depth_class[None, :], speed_rows, field)

    mine = lax.all_to_all(moved, "dir", split_axis=0, concat_axis=0, tiled=True)
    start = group * cols
    turn = lax.dynamic_slice_in_dim(refraction, start, cols)[None, :]
    my_mask = lax.dynamic_slice_in_dim(mask, start, cols)[None, :]
    weights = jnp.tile(wave_weight, total_dirs)[:, None]
    moved_cost = 2 * count * count * cols * 3 * SUB
    result = pl.pallas_call(
        functools.partial(source_kernel, freqs, groups),
        out_shape=jax.ShapeDtypeStruct((rows, points), F32),
        in_specs=[whole()] * 5,
        out_specs=whole(),
        scratch_shapes=[
            pltpu.VMEM((count // 2, count), F32),
            pltpu.VMEM((count, count), BF16),
            pltpu.VMEM((count, count), BF16),
            pltpu.VMEM((count, cols), F32),
            pltpu.VMEM((count, cols), BF16),
            pltpu.VMEM((count, cols), BF16),
            pltpu.VMEM((groups, rows, cols), F32),
            pltpu.SemaphoreType.DMA((2,)),
            pltpu.SemaphoreType.DMA((2,)),
            pltpu.SemaphoreType.DMA((groups,)),
            pltpu.SemaphoreType.DMA((groups,)),
        ],
        compiler_params=pltpu.CompilerParams(
            vmem_limit_bytes=58 * 2**20, collective_id=0, has_side_effects=True
        ),
        cost_estimate=pl.CostEstimate(flops=moved_cost, bytes_accessed=4 * count * count, transcendentals=0),
        name="source",
    )(mine.reshape(count, cols), turn, my_mask, weights, half)
    return result.reshape(dirs_local, freqs, points)


def solution(mesh):
    return jax.shard_map(
        per_device,
        mesh=mesh,
        in_specs=(
            P("dir", None, "tile"),
            P("tile"),
            P("tile", None, None),
            P(None, "tile"),
            P("tile"),
            P(),
            P("tile"),
            P("dir", None),
            P(),
        ),
        out_specs=P("dir", None, "tile"),
        check_vma=False,
    )
```

```python
import functools
import math

import jax
import jax.numpy as jnp
from jax import lax
from jax.experimental import pallas as pl
from jax.experimental.pallas import tpu as pltpu
from jax.sharding import PartitionSpec as P

SUB = 5
F32 = jnp.float32
BF16 = jnp.bfloat16


def split2(x):
    hi = x.astype(BF16)
    return hi, (x - hi.astype(F32)).astype(BF16)


def pick_kernel(ext_ref, send_ref, out_ref):
    points = ext_ref.shape[1]
    want = lax.broadcasted_iota(jnp.int32, (points, send_ref.shape[1]), 0)
    pick = jnp.where(want == send_ref[...], 1.0, 0.0).astype(BF16)
    total = None
    rest = ext_ref[...]
    for _ in range(3):
        part = rest.astype(BF16)
        rest = rest - part.astype(F32)
        got = jnp.dot(part, pick, preferred_element_type=F32)
        total = got if total is None else total + got
    out_ref[...] = total


def move_kernel(ways, field_ref, halo_ref, idx_ref, up_ref, depth_ref, speed_ref, block_ref, out_ref, parts_ref):
    rows, points = field_ref.shape
    width = points + halo_ref.shape[1]

    @pl.when(pl.program_id(0) == 0)
    def _():
        for ref, lo in ((field_ref, 0), (halo_ref, points)):
            hi_part, lo_part = split2(ref[...])
            parts_ref[0, :, lo:lo + ref.shape[1]] = hi_part
            parts_ref[1, :, lo:lo + ref.shape[1]] = lo_part

    own = block_ref[...]
    cols = own.shape[1]
    number = lax.broadcasted_iota(jnp.int32, (width, cols), 0)
    flow = None
    for k in range(ways):
        pick = jnp.where(number == idx_ref[k:k + 1, :], 1.0, 0.0).astype(BF16)
        got = jnp.dot(parts_ref[0], pick, preferred_element_type=F32)
        got = got + jnp.dot(parts_ref[1], pick, preferred_element_type=F32)
        term = up_ref[:, k:k + 1] * (got - own)
        flow = term if flow is None else flow + term
    courant = None
    for c in range(speed_ref.shape[1]):
        term = speed_ref[:, c:c + 1] * jnp.where(depth_ref[...] == c, 1.0, 0.0)
        courant = term if courant is None else courant + term
    out_ref[0] = own + courant * flow


def source_kernel(
    freqs, groups, moved_ref, turn_ref, mask_ref, weight_ref, half_ref, out_ref,
    other_ref, khi_ref, klo_ref, state_ref, shi_ref, slo_ref, done_ref,
    half_send, half_recv, send_sem, recv_sem,
):
    count, points = state_ref.shape
    rows = count // groups
    half = count // 2
    size = half // 2
    me = lax.axis_index("dir")
    parity = lax.rem(me, 2)
    twin = me + 1 - 2 * parity

    barrier = pltpu.get_barrier_semaphore()
    for r in range(1, groups):
        pl.semaphore_signal(barrier, inc=1, device_id={"dir": lax.rem(me + r, groups)}, device_id_type=pl.DeviceIdType.MESH)
    pl.semaphore_wait(barrier, groups - 1)

    copies = []
    for i in range(2):
        copy = pltpu.make_async_remote_copy(
            src_ref=half_ref.at[pl.ds(i * size, size)],
            dst_ref=other_ref.at[pl.ds(i * size, size)],
            send_sem=half_send.at[i],
            recv_sem=half_recv.at[i],
            device_id={"dir": twin},
            device_id_type=pl.DeviceIdType.MESH,
        )
        copy.start()
        copies.append(copy)

    def split_rows(ref, i, base):
        hi, lo = split2(ref[i * size:(i + 1) * size, :])
        to = pl.ds(pl.multiple_of(base * half + i * size, 16), size)
        khi_ref[to, :] = hi
        klo_ref[to, :] = lo

    moved = moved_ref[...]
    forward = jnp.maximum(turn_ref[...], 0.0)
    backward = jnp.maximum(-turn_ref[...], 0.0)
    lower = pltpu.roll(moved, freqs, 0)
    upper = pltpu.roll(moved, count - freqs, 0)
    state_ref[...] = moved + forward * (lower - moved) + backward * (upper - moved)
    for i in range(2):
        split_rows(half_ref, i, parity)
    for i in range(2):
        copies[i].wait()
        split_rows(other_ref, i, 1 - parity)

    def send(target):
        return pltpu.make_async_remote_copy(
            src_ref=done_ref.at[target],
            dst_ref=out_ref.at[:, pl.ds(pl.multiple_of(me * points, points), points)],
            send_sem=send_sem.at[target],
            recv_sem=recv_sem.at[me],
            device_id={"dir": target},
            device_id_type=pl.DeviceIdType.MESH,
        )

    def substep(last):
        state = state_ref[...]
        steep = jnp.sum(weight_ref[...] * (state * state), axis=0, keepdims=True)
        scale = 1.0 / (1.0 + steep)
        if last:
            scale = scale * mask_ref[...]
        hi, lo = split2(state)
        shi_ref[...] = hi
        slo_ref[...] = lo
        for h in range(2):
            khi = khi_ref[h * half:(h + 1) * half, :]
            product = jnp.dot(khi, shi_ref[...], preferred_element_type=F32)
            product = product + jnp.dot(khi, slo_ref[...], preferred_element_type=F32)
            product = product + jnp.dot(klo_ref[h * half:(h + 1) * half, :], shi_ref[...], preferred_element_type=F32)
            for j in range(groups // 2):
                d = 2 * j + h
                value = (state_ref[d * rows:(d + 1) * rows, :] + product[j * rows:(j + 1) * rows]) * scale
                if last:
                    done_ref[d] = value
                else:
                    state_ref[d * rows:(d + 1) * rows, :] = value
            if last:
                for j in range(groups // 2):
                    target = 2 * lax.rem(me // 2 + 1 + j, groups // 2) + h

                    @pl.when(target != me)
                    def _():
                        send(target).start()

    @pl.loop(0, SUB - 1)
    def _(step):
        substep(False)

    substep(True)
    out_ref[:, pl.ds(pl.multiple_of(me * points, points), points)] = done_ref[me]
    for r in range(1, groups):
        other = lax.rem(me + r, groups)
        send(other).wait_send()
        pltpu.make_async_remote_copy(
            src_ref=done_ref.at[other],
            dst_ref=out_ref.at[:, pl.ds(pl.multiple_of(other * points, points), points)],
            send_sem=send_sem.at[other],
            recv_sem=recv_sem.at[other],
            device_id={"dir": other},
            device_id_type=pl.DeviceIdType.MESH,
        ).wait_recv()


def per_device(
    spectrum,
    active_points,
    send_list,
    neighbor,
    depth_class,
    group_speed,
    refraction,
    kernel,
    wave_weight,
):
    dirs_local, freqs, points = spectrum.shape
    tiles = lax.axis_size("tile")
    groups = lax.axis_size("dir")
    faces = send_list.shape[2]
    classes = group_speed.shape[0]
    rows = dirs_local * freqs
    count = rows * groups
    cols = points // groups
    total_dirs = dirs_local * groups
    group = lax.axis_index("dir")
    vmem = pltpu.CompilerParams(vmem_limit_bytes=56 * 2**20)
    whole = functools.partial(pl.BlockSpec, memory_space=pltpu.VMEM)

    slots = groups // 2
    twos = slots & (slots - 1) == 0
    blocks = [(group // 2, kernel)]
    for k in range(1, slots):
        route = [(i, 2 * (((i // 2) ^ k) if twos else (i // 2 + k) % slots) + i % 2) for i in range(groups)]
        came = lax.ppermute(kernel, "dir", route)
        place = (group // 2) ^ k if twos else (group // 2 + slots - k) % slots
        blocks.append((place, came))

    mask = (jnp.arange(points, dtype=jnp.int32) < active_points[0]).astype(F32)
    field = spectrum.reshape(rows, points) * mask[None, :]
    send = send_list.reshape(1, tiles * faces)
    outgoing = pl.pallas_call(
        pick_kernel,
        out_shape=jax.ShapeDtypeStruct((rows, tiles * faces), F32),
        in_specs=[whole(), whole()],
        out_specs=whole(),
        compiler_params=vmem,
        name="pick",
    )(field, send)
    incoming = lax.all_to_all(outgoing, "tile", split_axis=1, concat_axis=1, tiled=True)

    first_dir = group * dirs_local
    theta = (first_dir + jnp.arange(dirs_local, dtype=jnp.int32)).astype(F32) * (2.0 * math.pi / total_dirs)
    angles = jnp.arange(4).astype(F32) * (math.pi / 2.0)
    upwind = jnp.maximum(jnp.cos(theta[:, None] - angles[None, :]), 0.0)
    links = neighbor
    ways = 4
    quarter = total_dirs // 4
    if total_dirs % 4 == 0 and quarter % dirs_local == 0:
        k0 = first_dir // quarter
        pair = jnp.stack([k0, (k0 + 1) % 4])
        upwind = jnp.take(upwind, pair, axis=1)
        links = jnp.take(neighbor, pair, axis=0)
        ways = 2
    up_rows = jnp.repeat(upwind, freqs, axis=0)
    speed_rows = jnp.tile(group_speed.T, (dirs_local, 1))

    moved = pl.pallas_call(
        functools.partial(move_kernel, ways),
        grid=(groups,),
        out_shape=jax.ShapeDtypeStruct((groups, rows, cols), F32),
        in_specs=[
            whole(),
            whole(),
            pl.BlockSpec((ways, cols), lambda i: (0, i)),
            whole(),
            pl.BlockSpec((1, cols), lambda i: (0, i)),
            whole(),
            pl.BlockSpec((rows, cols), lambda i: (0, i)),
        ],
        out_specs=pl.BlockSpec((1, rows, cols), lambda i: (i, 0, 0)),
        scratch_shapes=[pltpu.VMEM((2, rows, points + tiles * faces), BF16)],
        compiler_params=vmem,
        name="move",
    )(field, incoming, links, up_rows, depth_class[None, :], speed_rows, field)

    mine = lax.all_to_all(moved, "dir", split_axis=0, concat_axis=0, tiled=True)
    start = group * cols
    turn = lax.dynamic_slice_in_dim(refraction, start, cols)[None, :]
    my_mask = lax.dynamic_slice_in_dim(mask, start, cols)[None, :]
    weights = jnp.tile(wave_weight, total_dirs)[:, None]
    half = jnp.zeros((count // 2, count), F32)
    for place, block in blocks:
        half = lax.dynamic_update_slice_in_dim(half, block, place * rows, 0)
    moved_cost = 2 * count * count * cols * 3 * SUB
    result = pl.pallas_call(
        functools.partial(source_kernel, freqs, groups),
        out_shape=jax.ShapeDtypeStruct((rows, points), F32),
        in_specs=[whole()] * 5,
        out_specs=whole(),
        scratch_shapes=[
            pltpu.VMEM((count // 2, count), F32),
            pltpu.VMEM((count, count), BF16),
            pltpu.VMEM((count, count), BF16),
            pltpu.VMEM((count, cols), F32),
            pltpu.VMEM((count, cols), BF16),
            pltpu.VMEM((count, cols), BF16),
            pltpu.VMEM((groups, rows, cols), F32),
            pltpu.SemaphoreType.DMA((2,)),
            pltpu.SemaphoreType.DMA((2,)),
            pltpu.SemaphoreType.DMA((groups,)),
            pltpu.SemaphoreType.DMA((groups,)),
        ],
        compiler_params=pltpu.CompilerParams(
            vmem_limit_bytes=58 * 2**20, collective_id=0, has_side_effects=True
        ),
        cost_estimate=pl.CostEstimate(flops=moved_cost, bytes_accessed=4 * count * count, transcendentals=0),
        name="source",
    )(mine.reshape(count, cols), turn, my_mask, weights, half)
    return result.reshape(dirs_local, freqs, points)


def solution(mesh):
    return jax.shard_map(
        per_device,
        mesh=mesh,
        in_specs=(
            P("dir", None, "tile"),
            P("tile"),
            P("tile", None, None),
            P(None, "tile"),
            P("tile"),
            P(),
            P("tile"),
            P("dir", None),
            P(),
        ),
        out_specs=P("dir", None, "tile"),
        check_vma=False,
    )
```

```python
import functools
import math

import jax
import jax.numpy as jnp
from jax import lax
from jax.experimental import pallas as pl
from jax.experimental.pallas import tpu as pltpu
from jax.sharding import PartitionSpec as P

SUB = 5
F32 = jnp.float32
BF16 = jnp.bfloat16


def split2(x):
    hi = x.astype(BF16)
    return hi, (x - hi.astype(F32)).astype(BF16)


def pick_kernel(ext_ref, send_ref, out_ref):
    points = ext_ref.shape[1]
    want = lax.broadcasted_iota(jnp.int32, (points, send_ref.shape[1]), 0)
    pick = jnp.where(want == send_ref[...], 1.0, 0.0).astype(BF16)
    total = None
    rest = ext_ref[...]
    for _ in range(3):
        part = rest.astype(BF16)
        rest = rest - part.astype(F32)
        got = jnp.dot(part, pick, preferred_element_type=F32)
        total = got if total is None else total + got
    out_ref[...] = total


def move_kernel(ways, field_ref, halo_ref, idx_ref, up_ref, depth_ref, speed_ref, block_ref, out_ref, parts_ref):
    rows, points = field_ref.shape
    width = points + halo_ref.shape[1]

    @pl.when(pl.program_id(0) == 0)
    def _():
        for ref, lo in ((field_ref, 0), (halo_ref, points)):
            hi_part, lo_part = split2(ref[...])
            parts_ref[0, :, lo:lo + ref.shape[1]] = hi_part
            parts_ref[1, :, lo:lo + ref.shape[1]] = lo_part

    own = block_ref[...]
    cols = own.shape[1]
    number = lax.broadcasted_iota(jnp.int32, (width, cols), 0)
    flow = None
    for k in range(ways):
        pick = jnp.where(number == idx_ref[k:k + 1, :], 1.0, 0.0).astype(BF16)
        got = jnp.dot(parts_ref[0], pick, preferred_element_type=F32)
        got = got + jnp.dot(parts_ref[1], pick, preferred_element_type=F32)
        term = up_ref[:, k:k + 1] * (got - own)
        flow = term if flow is None else flow + term
    courant = None
    for c in range(speed_ref.shape[1]):
        term = speed_ref[:, c:c + 1] * jnp.where(depth_ref[...] == c, 1.0, 0.0)
        courant = term if courant is None else courant + term
    out_ref[0] = own + courant * flow


def source_kernel(
    freqs, groups, moved_ref, turn_ref, mask_ref, weight_ref, half_ref, other_ref, out_ref,
    khi_ref, klo_ref, state_ref, shi_ref, slo_ref, done_ref,
    send_sem, recv_sem,
):
    count, points = state_ref.shape
    rows = count // groups
    half = count // 2
    size = half // 2
    me = lax.axis_index("dir")
    parity = lax.rem(me, 2)

    barrier = pltpu.get_barrier_semaphore()
    for r in range(1, groups):
        pl.semaphore_signal(barrier, inc=1, device_id={"dir": lax.rem(me + r, groups)}, device_id_type=pl.DeviceIdType.MESH)
    pl.semaphore_wait(barrier, groups - 1)

    def split_rows(ref, i, base):
        hi, lo = split2(ref[i * size:(i + 1) * size, :])
        to = pl.ds(pl.multiple_of(base * half + i * size, 16), size)
        khi_ref[to, :] = hi
        klo_ref[to, :] = lo

    moved = moved_ref[...]
    forward = jnp.maximum(turn_ref[...], 0.0)
    backward = jnp.maximum(-turn_ref[...], 0.0)
    lower = pltpu.roll(moved, freqs, 0)
    upper = pltpu.roll(moved, count - freqs, 0)
    state_ref[...] = moved + forward * (lower - moved) + backward * (upper - moved)
    for i in range(2):
        split_rows(half_ref, i, parity)
    for i in range(2):
        split_rows(other_ref, i, 1 - parity)

    def send(target):
        return pltpu.make_async_remote_copy(
            src_ref=done_ref.at[target],
            dst_ref=out_ref.at[:, pl.ds(pl.multiple_of(me * points, points), points)],
            send_sem=send_sem.at[target],
            recv_sem=recv_sem.at[me],
            device_id={"dir": target},
            device_id_type=pl.DeviceIdType.MESH,
        )

    def substep(last):
        state = state_ref[...]
        steep = jnp.sum(weight_ref[...] * (state * state), axis=0, keepdims=True)
        scale = 1.0 / (1.0 + steep)
        if last:
            scale = scale * mask_ref[...]
        hi, lo = split2(state)
        shi_ref[...] = hi
        slo_ref[...] = lo
        for h in range(2):
            khi = khi_ref[h * half:(h + 1) * half, :]
            product = jnp.dot(khi, shi_ref[...], preferred_element_type=F32)
            product = product + jnp.dot(khi, slo_ref[...], preferred_element_type=F32)
            product = product + jnp.dot(klo_ref[h * half:(h + 1) * half, :], shi_ref[...], preferred_element_type=F32)
            for j in range(groups // 2):
                d = 2 * j + h
                value = (state_ref[d * rows:(d + 1) * rows, :] + product[j * rows:(j + 1) * rows]) * scale
                if last:
                    done_ref[d] = value
                else:
                    state_ref[d * rows:(d + 1) * rows, :] = value
            if last:
                for j in range(groups // 2):
                    target = 2 * lax.rem(me // 2 + 1 + j, groups // 2) + h

                    @pl.when(target != me)
                    def _():
                        send(target).start()

    @pl.loop(0, SUB - 1)
    def _(step):
        substep(False)

    substep(True)
    out_ref[:, pl.ds(pl.multiple_of(me * points, points), points)] = done_ref[me]
    for r in range(1, groups):
        other = lax.rem(me + r, groups)
        send(other).wait_send()
        pltpu.make_async_remote_copy(
            src_ref=done_ref.at[other],
            dst_ref=out_ref.at[:, pl.ds(pl.multiple_of(other * points, points), points)],
            send_sem=send_sem.at[other],
            recv_sem=recv_sem.at[other],
            device_id={"dir": other},
            device_id_type=pl.DeviceIdType.MESH,
        ).wait_recv()


def per_device(
    spectrum,
    active_points,
    send_list,
    neighbor,
    depth_class,
    group_speed,
    refraction,
    kernel,
    wave_weight,
):
    dirs_local, freqs, points = spectrum.shape
    tiles = lax.axis_size("tile")
    groups = lax.axis_size("dir")
    faces = send_list.shape[2]
    classes = group_speed.shape[0]
    rows = dirs_local * freqs
    count = rows * groups
    cols = points // groups
    total_dirs = dirs_local * groups
    group = lax.axis_index("dir")
    vmem = pltpu.CompilerParams(vmem_limit_bytes=56 * 2**20)
    whole = functools.partial(pl.BlockSpec, memory_space=pltpu.VMEM)

    slots = groups // 2
    twos = slots & (slots - 1) == 0
    blocks = [(group // 2, kernel)]
    for k in range(1, slots):
        route = [(i, 2 * (((i // 2) ^ k) if twos else (i // 2 + k) % slots) + i % 2) for i in range(groups)]
        came = lax.ppermute(kernel, "dir", route)
        place = (group // 2) ^ k if twos else (group // 2 + slots - k) % slots
        blocks.append((place, came))

    mask = (jnp.arange(points, dtype=jnp.int32) < active_points[0]).astype(F32)
    field = spectrum.reshape(rows, points) * mask[None, :]
    send = send_list.reshape(1, tiles * faces)
    outgoing = pl.pallas_call(
        pick_kernel,
        out_shape=jax.ShapeDtypeStruct((rows, tiles * faces), F32),
        in_specs=[whole(), whole()],
        out_specs=whole(),
        compiler_params=vmem,
        name="pick",
    )(field, send)
    incoming = lax.all_to_all(outgoing, "tile", split_axis=1, concat_axis=1, tiled=True)

    first_dir = group * dirs_local
    theta = (first_dir + jnp.arange(dirs_local, dtype=jnp.int32)).astype(F32) * (2.0 * math.pi / total_dirs)
    angles = jnp.arange(4).astype(F32) * (math.pi / 2.0)
    upwind = jnp.maximum(jnp.cos(theta[:, None] - angles[None, :]), 0.0)
    links = neighbor
    ways = 4
    quarter = total_dirs // 4
    if total_dirs % 4 == 0 and quarter % dirs_local == 0:
        k0 = first_dir // quarter
        pair = jnp.stack([k0, (k0 + 1) % 4])
        upwind = jnp.take(upwind, pair, axis=1)
        links = jnp.take(neighbor, pair, axis=0)
        ways = 2
    up_rows = jnp.repeat(upwind, freqs, axis=0)
    speed_rows = jnp.tile(group_speed.T, (dirs_local, 1))

    moved = pl.pallas_call(
        functools.partial(move_kernel, ways),
        grid=(groups,),
        out_shape=jax.ShapeDtypeStruct((groups, rows, cols), F32),
        in_specs=[
            whole(),
            whole(),
            pl.BlockSpec((ways, cols), lambda i: (0, i)),
            whole(),
            pl.BlockSpec((1, cols), lambda i: (0, i)),
            whole(),
            pl.BlockSpec((rows, cols), lambda i: (0, i)),
        ],
        out_specs=pl.BlockSpec((1, rows, cols), lambda i: (i, 0, 0)),
        scratch_shapes=[pltpu.VMEM((2, rows, points + tiles * faces), BF16)],
        compiler_params=vmem,
        name="move",
    )(field, incoming, links, up_rows, depth_class[None, :], speed_rows, field)

    moved, half = lax.optimization_barrier((moved, jnp.zeros((count // 2, count), F32)))
    mine = lax.all_to_all(moved, "dir", split_axis=0, concat_axis=0, tiled=True)
    start = group * cols
    turn = lax.dynamic_slice_in_dim(refraction, start, cols)[None, :]
    my_mask = lax.dynamic_slice_in_dim(mask, start, cols)[None, :]
    weights = jnp.tile(wave_weight, total_dirs)[:, None]
    for place, block in blocks:
        half = lax.dynamic_update_slice_in_dim(half, block, place * rows, 0)
    other = lax.ppermute(half, "dir", [(i, i ^ 1) for i in range(groups)])
    moved_cost = 2 * count * count * cols * 3 * SUB
    result = pl.pallas_call(
        functools.partial(source_kernel, freqs, groups),
        out_shape=jax.ShapeDtypeStruct((rows, points), F32),
        in_specs=[whole()] * 6,
        out_specs=whole(),
        scratch_shapes=[
            pltpu.VMEM((count, count), BF16),
            pltpu.VMEM((count, count), BF16),
            pltpu.VMEM((count, cols), F32),
            pltpu.VMEM((count, cols), BF16),
            pltpu.VMEM((count, cols), BF16),
            pltpu.VMEM((groups, rows, cols), F32),
            pltpu.SemaphoreType.DMA((groups,)),
            pltpu.SemaphoreType.DMA((groups,)),
        ],
        compiler_params=pltpu.CompilerParams(
            vmem_limit_bytes=58 * 2**20, collective_id=0, has_side_effects=True
        ),
        cost_estimate=pl.CostEstimate(flops=moved_cost, bytes_accessed=4 * count * count, transcendentals=0),
        name="source",
    )(mine.reshape(count, cols), turn, my_mask, weights, half, other)
    return result.reshape(dirs_local, freqs, points)


def solution(mesh):
    return jax.shard_map(
        per_device,
        mesh=mesh,
        in_specs=(
            P("dir", None, "tile"),
            P("tile"),
            P("tile", None, None),
            P(None, "tile"),
            P("tile"),
            P(),
            P("tile"),
            P("dir", None),
            P(),
        ),
        out_specs=P("dir", None, "tile"),
        check_vma=False,
    )
```
